32 devices in a mesh: band: 4 (over y, x), kpt: 8 (over z, core).
Axes of the slice: x: 2, y: 2, z: 4, core: 2. Of those that a mesh axis runs over, the one named last changes fastest.
Arguments:
- orbitals: bfloat16 [4, 8, 2, 32, 1024], P('band', 'kpt'), may hold values from -6 to 6
- kcoord: int32 [8, 3], replicated, may hold values from 0 to 7
Outputs:
- exchange: float32 [4, 8, 2, 32, 1024], P('band', 'kpt')
The draws below stay inside these ranges and needn't reach their ends.
All inputs are finite; a program needn't handle non-finite values.
Results may differ from the reference program's by a relative error of at most 0.0003.
Values may be sent and summed in bfloat16 or wider, within the bound.
A program may use at most 64 MiB of HBM per device.

```python
import jax
import jax.numpy as jnp
from jax import lax

GRID = 32
BANDS = 4
KPTS = 8


def place_ends(array, stream_key, smallest, high):
    longest = array.shape.index(max(array.shape))
    spots = []
    for shift in (0, 1):
        where = [jax.random.randint(jax.random.fold_in(stream_key, axis), (), 0, length) for axis, length in enumerate(array.shape)]
        where[longest] = (where[longest] + shift) % array.shape[longest]
        spots.append(tuple(where))
    return array.at[spots[0]].set(smallest).at[spots[1]].set(high)


def levels(rng, shape, shards, low, top_value):
    gain, own = 1.0, jax.random.fold_in(rng, 6)
    for axis_at, parts in shards:
        heights = jnp.exp(jax.random.uniform(jax.random.fold_in(own, axis_at), (parts,), jnp.float32, low / len(shards), top_value / len(shards)))
        gain = gain * jnp.repeat(heights, shape[axis_at] // parts).reshape([-1 if axis == axis_at else 1 for axis in range(len(shape))])
    return gain


def gaussian(key, dims, spread, limit, pieces=(), kind=jnp.bfloat16):
    entries = jax.random.normal(key, dims, jnp.float32) * spread
    if len(pieces) > 0:
        entries = levels(key, dims, pieces, -0.22, 0.18) * entries
    return jnp.clip(entries, min=-limit, max=limit).astype(kind)


def setup_inputs(seed: int = 0) -> dict:
    splits = jax.random.split(jax.random.key(seed), 3)
    return {
        "orbitals": gaussian(splits[0], (BANDS, KPTS, 2, GRID, GRID * GRID), 1.0, 6.0, ((0, 4), (1, 8))),
        "kcoord": place_ends(jax.random.randint(splits[1], (KPTS, 3), 0, 8), jax.random.fold_in(splits[1], 1), 0, 7).astype(jnp.int32),
    }


def freq_grid(grid):
    line = jnp.arange(grid, dtype=jnp.int32)
    folded = ((line + grid // 2) % grid) - grid // 2
    return folded.astype(jnp.float32)


def kernel_for(grid, qvec):
    freq = freq_grid(grid)
    fx = (freq + qvec[0])[:, None, None]
    fy = (freq + qvec[1])[None, :, None]
    fz = (freq + qvec[2])[None, None, :]
    return 1.0 / (1.0 + (fx * fx + fy * fy + fz * fz) / 256.0)


def as_complex(field, grid):
    values = field.astype(jnp.float32).reshape(2, grid, grid, grid)
    return values[0] + 1j * values[1]


def pair_term(partner, own, kern):
    rho = jnp.conj(partner) * own
    phi = jnp.fft.ifftn(kern * jnp.fft.fftn(rho))
    return partner * phi


def reference(orbitals, kcoord):
    grid = orbitals.shape[3]
    bands = orbitals.shape[0]
    kpts = orbitals.shape[1]
    zero_q = jnp.zeros((3,), jnp.float32)
    kern_zero = kernel_for(grid, zero_q)

    def one(index):
        band_at = index // kpts
        kpt_at = index % kpts
        own = as_complex(orbitals[band_at, kpt_at], grid)
        total = jnp.zeros_like(own)
        for shift_by in (-2, -1, 1, 2):
            partner = as_complex(orbitals[(band_at + shift_by) % bands, kpt_at], grid)
            total = total + pair_term(partner, own, kern_zero)
        next_k = (kpt_at + 1) % kpts
        qvec = (kcoord[next_k] - kcoord[kpt_at]).astype(jnp.float32)
        partner = as_complex(orbitals[band_at, next_k], grid)
        total = total + pair_term(partner, own, kernel_for(grid, qvec))
        total = -total
        return jnp.stack([jnp.real(total), jnp.imag(total)]).reshape(2, grid, grid * grid)

    flat = lax.map(one, jnp.arange(bands * kpts, dtype=jnp.int32))
    return flat.reshape(bands, kpts, 2, grid, grid * grid)
```

```python
import functools
import math

import jax
import jax.numpy as jnp
import numpy as np
from jax import lax
from jax.experimental import pallas as pl
from jax.experimental.pallas import tpu as pltpu
from jax.sharding import PartitionSpec as P

MESH = pl.DeviceIdType.MESH


def real_basis(grid, parity, freqs, points):
    angle = 2.0 * math.pi / grid * (np.outer(freqs, points) % grid)
    if parity == 0:
        return np.cos(angle)
    rows = np.sin(angle)
    for at, freq in enumerate(freqs):
        if freq == 0:
            rows[at] = np.cos(math.pi * np.asarray(points))
    return rows


def split(table):
    table = np.asarray(table, np.float32)
    high = table.astype(jnp.bfloat16)
    low = (table - high.astype(np.float32)).astype(jnp.bfloat16)
    return [high, low]


def groups(grid):
    half = grid // 2
    odd = list(range(1, half, 2))
    return [list(range(0, half, 4)), list(range(2, half, 4)), odd[: len(odd) // 2], odd[len(odd) // 2 :]]


def plane_table(grid, freqs, points):
    zline = list(range(grid))
    half = list(range(grid // 2))
    parts = []
    for yp in (0, 1):
        for zp in (0, 1):
            parts.append(np.kron(real_basis(grid, yp, freqs, points), real_basis(grid, zp, half, zline)).T)
    return np.concatenate(parts, axis=1)


def tables(grid):
    eighth = list(range(grid // 4))
    quarter = groups(grid)
    a = plane_table(grid, quarter[0], eighth)
    b = plane_table(grid, quarter[1], eighth)
    odd_points = list(range(grid // 2))
    c = np.concatenate([plane_table(grid, quarter[2], odd_points), plane_table(grid, quarter[3], odd_points)], axis=1)
    half = list(range(grid // 2))
    line = list(range(grid))
    x = np.concatenate([real_basis(grid, 0, half, line), real_basis(grid, 1, half, line)], axis=0)
    x = np.kron(np.eye(8), x)
    small = np.stack([t for m in (a, a.T, b, b.T, x, x.T) for t in split(m)])
    large = np.stack([t for m in (c, c.T) for t in split(m)])
    return small, large


def lane_table(grid):
    half = grid // 2
    rows = []
    for freqs in groups(grid):
        fy, fz = [], []
        for yp in (0, 1):
            for zp in (0, 1):
                for j in freqs:
                    for i in range(half):
                        fy.append(j if yp == 0 else (-j if j else -half))
                        fz.append(i if zp == 0 else (-i if i else -half))
        fy, fz = np.array(fy), np.array(fz)
        paired = [(f != 0) & (f != -half) for f in (fy, fz)]
        rows.append(np.stack([fy, fz, paired[0], paired[1]] + [np.zeros_like(fy)] * 4))
    return np.stack(rows).astype(np.float32)


def halves(a):
    high = a.astype(jnp.bfloat16)
    low = (a - high.astype(jnp.float32)).astype(jnp.bfloat16)
    return high, low


def dot(a, b):
    return jnp.dot(a, b, preferred_element_type=jnp.float32)


def right(a, high_table, low_table):
    high, low = halves(a)
    rows = a.shape[0]
    both = dot(jnp.concatenate([high, low], axis=0), high_table)
    return both[:rows] + (both[rows:] + dot(high, low_table))


def left(high_table, low_table, a):
    high, low = halves(a)
    return dot(high_table, high) + (dot(low_table, high) + dot(high_table, low))


def x_freq(grid, shape):
    half = grid // 2
    row = lax.broadcasted_iota(jnp.int32, shape, len(shape) - 2)
    freq = jnp.where(row < half, row, jnp.where(row == half, -half, half - row))
    return freq.astype(jnp.float32), jnp.where(row % half == 0, 0.0, 1.0).astype(jnp.float32)


def swap_x(a):
    half = a.shape[1] // 2
    return jnp.concatenate([a[:, half:], a[:, :half]], axis=1)


def swap_y(a):
    half = a.shape[2] // 2
    return jnp.concatenate([a[:, :, half:], a[:, :, :half]], axis=2)


def swap_z(a):
    half = a.shape[2] // 2
    parts = [pltpu.roll(a[:, :, at * half : (at + 1) * half], half // 2, 2) for at in (0, 1)]
    return jnp.concatenate(parts, axis=2)


def convolve(parts, kern, small, large, pairing):
    rows, lanes = parts[0].shape
    grid = rows // 2
    sum_02, sum_13 = parts[0] + parts[2], parts[1] + parts[3]
    odd = jnp.concatenate([parts[0] - parts[2], parts[1] - parts[3]], axis=1)
    freq_a = right(sum_02 + sum_13, small[0], small[1])
    freq_b = right(sum_02 - sum_13, small[4], small[5])
    freq_c = right(odd, large[0], large[1])
    field = jnp.concatenate([freq_a, freq_b, freq_c[:, :lanes], freq_c[:, lanes:]], axis=0)
    field = left(small[8], small[9], field)
    if pairing is None:
        field = (field.reshape(4, 2, grid, lanes) * kern[:, None]).reshape(4 * rows, lanes)
    else:
        field = field.reshape(4, 2, grid, lanes)
        re, im = field[:, 0], field[:, 1]
        for swap, paired in zip((swap_x, swap_y, swap_z), pairing):
            re, im = re + paired * swap(im), im - paired * swap(re)
        re, im = re * kern, im * kern
        for swap, paired in zip((swap_x, swap_y, swap_z), pairing):
            re, im = re - paired * swap(im), im + paired * swap(re)
        field = jnp.stack([re, im], axis=1).reshape(4 * rows, lanes)
    field = left(small[10], small[11], field)
    back_a = right(field[:rows], small[2], small[3])
    back_b = right(field[rows : 2 * rows], small[6], small[7])
    back_c = right(jnp.concatenate([field[2 * rows : 3 * rows], field[3 * rows :]], axis=1), large[2], large[3])
    even, alternate = back_a + back_b, back_a - back_b
    return [even + back_c[:, :lanes], alternate + back_c[:, lanes:], even - back_c[:, :lanes], alternate - back_c[:, lanes:]]


def band_partners(bands):
    if bands == 4:
        flip = lambda b: b + 1 - 2 * (b % 2)
        across = lambda b: (b + 2) % 4
        corner = lambda b: 3 - b
        return [(flip, flip, 1.0), (across, across, 2.0), (corner, corner, 1.0)]
    counts = {}
    for shift in (1, -1, 2, -2):
        counts[shift % bands] = counts.get(shift % bands, 0) + 1
    found = []
    for shift, times in counts.items():
        found.append((lambda b, s=shift: (b + s) % bands, lambda b, s=shift: (b + bands - s) % bands, float(times)))
    return found


def kernel(bands, kpts, kcoord_ref, own_hbm, small_hbm, large_hbm, lane_ref, out_ref, own, got, small, large, local_sems, send_sems, recv_sems):
    band = lax.axis_index("band")
    kpt = lax.axis_index("kpt")
    partners = band_partners(bands)
    later, earlier = (kpt + 1) % kpts, (kpt + kpts - 1) % kpts
    sources = [(band, later)] + [(src(band), kpt) for src, _, _ in partners]
    targets = [(band, earlier)] + [(dst(band), kpt) for _, dst, _ in partners]
    greeted = [(band, later)] + ([(band, earlier)] if kpts > 2 else [])
    if bands == 4:
        greeted += sources[1:]
    else:
        greeted += [((band + s) % bands, kpt) for s in sorted({s % bands for s in (1, -1, 2, -2)})]

    barrier = pltpu.get_barrier_semaphore()
    for device in greeted:
        pl.semaphore_signal(barrier, inc=1, device_id=device, device_id_type=MESH)
    fetches = [
        pltpu.make_async_copy(own_hbm, own, local_sems.at[0]),
        pltpu.make_async_copy(small_hbm, small, local_sems.at[1]),
        pltpu.make_async_copy(large_hbm, large, local_sems.at[2]),
    ]
    for fetch in fetches:
        fetch.start()
    pl.semaphore_wait(barrier, len(greeted))
    copies = []
    for at, device in enumerate(targets):
        copies.append(
            pltpu.make_async_remote_copy(
                src_ref=own_hbm,
                dst_ref=got.at[at],
                send_sem=send_sems.at[at],
                recv_sem=recv_sems.at[at],
                device_id=device,
                device_id_type=MESH,
            )
        )
    for at in list(range(1, len(targets) - 1)) + [0, len(targets) - 1]:
        copies[at].start()

    grid = own_hbm.shape[1]
    lanes = own_hbm.shape[2] // 4
    scale = -1.0 / float(grid**3)
    fx, x_paired = x_freq(grid, (1, grid, lanes))
    fy, fz = lane_ref[:, 0:1, :], lane_ref[:, 1:2, :]
    y_paired, z_paired = lane_ref[:, 2:3, :], lane_ref[:, 3:4, :]
    qx, qy, qz = [(kcoord_ref[later, i] - kcoord_ref[kpt, i]).astype(jnp.float32) for i in range(3)]
    weight = (1.0 + x_paired) * ((1.0 + y_paired) * (1.0 + z_paired)) * scale
    kern_zero = weight / (1.0 + (fx * fx + fy * fy + fz * fz) / 256.0)
    gx, gy, gz = fx + qx, fy + qy, fz + qz
    kern_next = scale / (1.0 + (gx * gx + gy * gy + gz * gz) / 256.0)

    for fetch in fetches:
        fetch.wait()
    times = [1.0] + [t for _, _, t in partners]
    for at in range(len(targets)):
        copies[at].wait_recv()
        parts = []
        for part in range(4):
            cut = slice(part * lanes, (part + 1) * lanes)
            own_re, own_im = own[0, :, cut].astype(jnp.float32), own[1, :, cut].astype(jnp.float32)
            re, im = got[at, 0, :, cut].astype(jnp.float32), got[at, 1, :, cut].astype(jnp.float32)
            parts.append(jnp.concatenate([re * own_re + im * own_im, re * own_im - im * own_re], axis=0))
        if at == 0:
            phi = convolve(parts, kern_next, small, large, (x_paired, y_paired, z_paired))
        else:
            phi = convolve(parts, kern_zero * times[at], small, large, None)
        for part in range(4):
            cut = slice(part * lanes, (part + 1) * lanes)
            re, im = got[at, 0, :, cut].astype(jnp.float32), got[at, 1, :, cut].astype(jnp.float32)
            phi_re, phi_im = phi[part][:grid], phi[part][grid:]
            term_re = re * phi_re - im * phi_im
            term_im = re * phi_im + im * phi_re
            if at > 0:
                term_re = term_re + out_ref[0, :, cut]
                term_im = term_im + out_ref[1, :, cut]
            out_ref[0, :, cut] = term_re
            out_ref[1, :, cut] = term_im
    for copy in copies:
        copy.wait_send()


def local(bands, kpts, orbitals, kcoord):
    own = orbitals[0, 0]
    grid, merged = own.shape[1:]
    small, large = tables(grid)
    lanes = lane_table(grid)
    count = 1 + len(band_partners(bands))
    anywhere = pl.BlockSpec(memory_space=pl.ANY)
    vmem = pl.BlockSpec(memory_space=pltpu.VMEM)
    out = pl.pallas_call(
        functools.partial(kernel, bands, kpts),
        out_shape=jax.ShapeDtypeStruct((2, grid, merged), jnp.float32),
        in_specs=[pl.BlockSpec(memory_space=pltpu.SMEM), anywhere, anywhere, anywhere, vmem],
        out_specs=vmem,
        scratch_shapes=[
            pltpu.VMEM(own.shape, jnp.bfloat16),
            pltpu.VMEM((count, *own.shape), jnp.bfloat16),
            pltpu.VMEM(small.shape, jnp.bfloat16),
            pltpu.VMEM(large.shape, jnp.bfloat16),
            pltpu.SemaphoreType.DMA((3,)),
            pltpu.SemaphoreType.DMA((count,)),
            pltpu.SemaphoreType.DMA((count,)),
        ],
        compiler_params=pltpu.CompilerParams(collective_id=0, has_side_effects=True, vmem_limit_bytes=40 * 1024 * 1024),
    )(kcoord, own, jnp.asarray(small), jnp.asarray(large), jnp.asarray(lanes))
    return out.reshape(1, 1, 2, grid, merged)


def solution(mesh):
    in_specs = (P("band", "kpt", None, None, None), P())
    out_specs = P("band", "kpt", None, None, None)
    body = functools.partial(local, mesh.shape["band"], mesh.shape["kpt"])
    return jax.shard_map(body, mesh=mesh, in_specs=in_specs, out_specs=out_specs, check_vma=False)
```

```python
import functools
import math

import jax
import jax.numpy as jnp
import numpy as np
from jax import lax
from jax.experimental import pallas as pl
from jax.experimental.pallas import tpu as pltpu
from jax.sharding import PartitionSpec as P

MESH = pl.DeviceIdType.MESH
VMEM_BYTES = 56 * 1024 * 1024


def real_basis(grid, parity, freqs, points):
    angle = 2.0 * math.pi / grid * (np.outer(freqs, points) % grid)
    if parity == 0:
        return np.cos(angle)
    rows = np.sin(angle)
    for at, freq in enumerate(freqs):
        if freq == 0:
            rows[at] = np.cos(math.pi * np.asarray(points))
    return rows


def split(table):
    table = np.asarray(table, np.float32)
    high = table.astype(jnp.bfloat16)
    low = (table - high.astype(np.float32)).astype(jnp.bfloat16)
    return [high, low]


def groups(grid):
    half = grid // 2
    odd = list(range(1, half, 2))
    return [list(range(0, half, 4)), list(range(2, half, 4)), odd[: len(odd) // 2], odd[len(odd) // 2 :]]


def plane_table(grid, freqs, points):
    zline = list(range(grid))
    half = list(range(grid // 2))
    parts = []
    for yp in (0, 1):
        for zp in (0, 1):
            parts.append(np.kron(real_basis(grid, yp, freqs, points), real_basis(grid, zp, half, zline)).T)
    return np.concatenate(parts, axis=1)


def tables(grid):
    eighth = list(range(grid // 4))
    quarter = groups(grid)
    a = plane_table(grid, quarter[0], eighth)
    b = plane_table(grid, quarter[1], eighth)
    odd_points = list(range(grid // 2))
    c = np.concatenate([plane_table(grid, quarter[2], odd_points), plane_table(grid, quarter[3], odd_points)], axis=1)
    half = list(range(grid // 2))
    line = list(range(grid))
    x = np.concatenate([real_basis(grid, 0, half, line), real_basis(grid, 1, half, line)], axis=0)
    x = np.kron(np.eye(8), x)
    small = np.stack([t for m in (a, a.T, b, b.T, x, x.T) for t in split(m)])
    large = np.stack([t for m in (c, c.T) for t in split(m)])
    return small, large


def lane_freqs(grid):
    half, count = grid // 2, grid // 8
    shape = (4, 1, 4 * count * half)
    quarter = lax.broadcasted_iota(jnp.int32, shape, 0)
    lane = lax.broadcasted_iota(jnp.int32, shape, 2)
    at = (lane // half) % count
    y = jnp.where(quarter < 2, 4 * at + 2 * quarter, 2 * at + 1 + 2 * count * (quarter - 2))
    z = lane % half
    found = []
    for size, second in ((y, lane // (2 * count * half) > 0), (z, (lane // (count * half)) % 2 > 0)):
        freq = jnp.where(second, jnp.where(size == 0, -half, -size), size)
        found.append((freq.astype(jnp.float32), jnp.where(size == 0, 0.0, 1.0).astype(jnp.float32)))
    return found


def halves(a):
    high = a.astype(jnp.bfloat16)
    low = (a - high.astype(jnp.float32)).astype(jnp.bfloat16)
    return high, low


def dot(a, b):
    return jnp.dot(a, b, preferred_element_type=jnp.float32)


def right(a, high_table, low_table):
    high, low = halves(a)
    rows = a.shape[0]
    both = dot(jnp.concatenate([high, low], axis=0), high_table)
    return both[:rows] + (both[rows:] + dot(high, low_table))


def left(high_table, low_table, a):
    high, low = halves(a)
    return dot(high_table, high) + (dot(low_table, high) + dot(high_table, low))


def x_freq(grid, shape):
    half = grid // 2
    row = lax.broadcasted_iota(jnp.int32, shape, len(shape) - 2)
    freq = jnp.where(row < half, row, jnp.where(row == half, -half, half - row))
    return freq.astype(jnp.float32), jnp.where(row % half == 0, 0.0, 1.0).astype(jnp.float32)


def swap_x(a):
    half = a.shape[1] // 2
    return jnp.concatenate([a[:, half:], a[:, :half]], axis=1)


def swap_y(a):
    half = a.shape[2] // 2
    return jnp.concatenate([a[:, :, half:], a[:, :, :half]], axis=2)


def swap_z(a):
    half = a.shape[2] // 2
    parts = [pltpu.roll(a[:, :, at * half : (at + 1) * half], half // 2, 2) for at in (0, 1)]
    return jnp.concatenate(parts, axis=2)


def convolve(parts, kern, small, large, pairing):
    rows, lanes = parts[0].shape
    grid = rows // 2
    sum_02, sum_13 = parts[0] + parts[2], parts[1] + parts[3]
    odd = jnp.concatenate([parts[0] - parts[2], parts[1] - parts[3]], axis=1)
    freq_a = right(sum_02 + sum_13, small[0], small[1])
    freq_b = right(sum_02 - sum_13, small[4], small[5])
    freq_c = right(odd, large[0], large[1])
    field = jnp.concatenate([freq_a, freq_b, freq_c[:, :lanes], freq_c[:, lanes:]], axis=0)
    field = left(small[8], small[9], field)
    if pairing is None:
        field = (field.reshape(4, 2, grid, lanes) * kern[:, None]).reshape(4 * rows, lanes)
    else:
        field = field.reshape(4, 2, grid, lanes)
        re, im = field[:, 0], field[:, 1]
        for swap, paired in zip((swap_x, swap_y, swap_z), pairing):
            re, im = re + paired * swap(im), im - paired * swap(re)
        re, im = re * kern, im * kern
        for swap, paired in zip((swap_x, swap_y, swap_z), pairing):
            re, im = re - paired * swap(im), im + paired * swap(re)
        field = jnp.stack([re, im], axis=1).reshape(4 * rows, lanes)
    field = left(small[10], small[11], field)
    back_a = right(field[:rows], small[2], small[3])
    back_b = right(field[rows : 2 * rows], small[6], small[7])
    back_c = right(jnp.concatenate([field[2 * rows : 3 * rows], field[3 * rows :]], axis=1), large[2], large[3])
    even, alternate = back_a + back_b, back_a - back_b
    return [even + back_c[:, :lanes], alternate + back_c[:, lanes:], even - back_c[:, :lanes], alternate - back_c[:, lanes:]]


def band_partners(bands):
    if bands == 4:
        flip = lambda b: b + 1 - 2 * (b % 2)
        across = lambda b: (b + 2) % 4
        corner = lambda b: 3 - b
        return [(flip, flip, 1.0), (across, across, 2.0), (corner, corner, 1.0)]
    counts = {}
    for shift in (1, -1, 2, -2):
        counts[shift % bands] = counts.get(shift % bands, 0) + 1
    found = []
    for shift, times in counts.items():
        found.append((lambda b, s=shift: (b + s) % bands, lambda b, s=shift: (b + bands - s) % bands, float(times)))
    return found


def kernel(bands, kpts, kcoord_hbm, own_hbm, small_hbm, large_hbm, out_ref, kcoord_ref, own, got, small, large, local_sems, send_sems, recv_sems):
    band = lax.axis_index("band")
    kpt = lax.axis_index("kpt")
    partners = band_partners(bands)
    later, earlier = (kpt + 1) % kpts, (kpt + kpts - 1) % kpts
    sources = [(band, later)] + [(src(band), kpt) for src, _, _ in partners]
    targets = [(band, earlier)] + [(dst(band), kpt) for _, dst, _ in partners]
    greeted = [(band, later)] + ([(band, earlier)] if kpts > 2 else [])
    if bands == 4:
        greeted += sources[1:]
    else:
        greeted += [((band + s) % bands, kpt) for s in sorted({s % bands for s in (1, -1, 2, -2)})]

    barrier = pltpu.get_barrier_semaphore()
    for device in greeted:
        pl.semaphore_signal(barrier, inc=1, device_id=device, device_id_type=MESH)
    fetches = [
        pltpu.make_async_copy(own_hbm, own, local_sems.at[0]),
        pltpu.make_async_copy(small_hbm, small, local_sems.at[1]),
        pltpu.make_async_copy(large_hbm, large, local_sems.at[2]),
        pltpu.make_async_copy(kcoord_hbm, kcoord_ref, local_sems.at[3]),
    ]
    for fetch in fetches:
        fetch.start()
    pl.semaphore_wait(barrier, len(greeted))
    copies = []
    for at, device in enumerate(targets):
        copies.append(
            pltpu.make_async_remote_copy(
                src_ref=own_hbm,
                dst_ref=got.at[at],
                send_sem=send_sems.at[at],
                recv_sem=recv_sems.at[at],
                device_id=device,
                device_id_type=MESH,
            )
        )
    for at in list(range(1, len(targets) - 1)) + [0, len(targets) - 1]:
        copies[at].start()

    grid = own_hbm.shape[1]
    lanes = own_hbm.shape[2] // 4
    scale = -1.0 / float(grid**3)
    fx, x_paired = x_freq(grid, (1, grid, lanes))
    (fy, y_paired), (fz, z_paired) = lane_freqs(grid)
    for fetch in fetches:
        fetch.wait()
    qx, qy, qz = [(kcoord_ref[i, later] - kcoord_ref[i, kpt]).astype(jnp.float32) for i in range(3)]
    weight = (1.0 + x_paired) * ((1.0 + y_paired) * (1.0 + z_paired)) * scale
    kern_zero = weight / (1.0 + (fx * fx + fy * fy + fz * fz) / 256.0)
    gx, gy, gz = fx + qx, fy + qy, fz + qz
    kern_next = scale / (1.0 + (gx * gx + gy * gy + gz * gz) / 256.0)

    times = [1.0] + [t for _, _, t in partners]
    for at in range(len(targets)):
        copies[at].wait_recv()
        parts = []
        for part in range(4):
            cut = slice(part * lanes, (part + 1) * lanes)
            own_re, own_im = own[0, :, cut].astype(jnp.float32), own[1, :, cut].astype(jnp.float32)
            re, im = got[at, 0, :, cut].astype(jnp.float32), got[at, 1, :, cut].astype(jnp.float32)
            parts.append(jnp.concatenate([re * own_re + im * own_im, re * own_im - im * own_re], axis=0))
        if at == 0:
            phi = convolve(parts, kern_next, small, large, (x_paired, y_paired, z_paired))
        else:
            phi = convolve(parts, kern_zero * times[at], small, large, None)
        for part in range(4):
            cut = slice(part * lanes, (part + 1) * lanes)
            re, im = got[at, 0, :, cut].astype(jnp.float32), got[at, 1, :, cut].astype(jnp.float32)
            phi_re, phi_im = phi[part][:grid], phi[part][grid:]
            term_re = re * phi_re - im * phi_im
            term_im = re * phi_im + im * phi_re
            if at > 0:
                term_re = term_re + out_ref[0, :, cut]
                term_im = term_im + out_ref[1, :, cut]
            out_ref[0, :, cut] = term_re
            out_ref[1, :, cut] = term_im
    for copy in copies:
        copy.wait_send()


def local(bands, kpts, orbitals, kcoord):
    own = orbitals[0, 0]
    grid, merged = own.shape[1:]
    small, large = tables(grid)
    count = 1 + len(band_partners(bands))
    hbm = pl.BlockSpec(memory_space=pltpu.HBM)
    vmem = pl.BlockSpec(memory_space=pltpu.VMEM)
    out = pl.pallas_call(
        functools.partial(kernel, bands, kpts),
        out_shape=pltpu.VMEM((2, grid, merged), jnp.float32),
        in_specs=[hbm, hbm, hbm, hbm],
        out_specs=vmem,
        scratch_shapes=[
            pltpu.SMEM(kcoord.T.shape, jnp.int32),
            pltpu.VMEM(own.shape, jnp.bfloat16),
            pltpu.VMEM((count, *own.shape), jnp.bfloat16),
            pltpu.VMEM(small.shape, jnp.bfloat16),
            pltpu.VMEM(large.shape, jnp.bfloat16),
            pltpu.SemaphoreType.DMA((4,)),
            pltpu.SemaphoreType.DMA((count,)),
            pltpu.SemaphoreType.DMA((count,)),
        ],
        compiler_params=pltpu.CompilerParams(collective_id=0, has_side_effects=True, vmem_limit_bytes=VMEM_BYTES),
    )(kcoord.T, own, jnp.asarray(small), jnp.asarray(large))
    return out.reshape(1, 1, 2, grid, merged)


def solution(mesh):
    in_specs = (P("band", "kpt", None, None, None), P())
    out_specs = P("band", "kpt", None, None, None)
    body = functools.partial(local, mesh.shape["band"], mesh.shape["kpt"])
    return jax.shard_map(body, mesh=mesh, in_specs=in_specs, out_specs=out_specs, check_vma=False)
```

```python
import functools
import math

import jax
import jax.numpy as jnp
import numpy as np
from jax import lax
from jax.experimental import pallas as pl
from jax.experimental.pallas import tpu as pltpu
from jax.sharding import PartitionSpec as P

MESH = pl.DeviceIdType.MESH
VMEM_BYTES = 56 * 1024 * 1024


def real_basis(grid, parity, freqs, points):
    angle = 2.0 * math.pi / grid * (np.outer(freqs, points) % grid)
    if parity == 0:
        return np.cos(angle)
    rows = np.sin(angle)
    for at, freq in enumerate(freqs):
        if freq == 0:
            rows[at] = np.cos(math.pi * np.asarray(points))
    return rows


def split(table):
    table = np.asarray(table, np.float32)
    high = table.astype(jnp.bfloat16)
    low = (table - high.astype(np.float32)).astype(jnp.bfloat16)
    return [high, low]


def groups(grid):
    half = grid // 2
    odd = list(range(1, half, 2))
    return [list(range(0, half, 4)), list(range(2, half, 4)), odd[: len(odd) // 2], odd[len(odd) // 2 :]]


def plane_table(grid, freqs, points):
    zline = list(range(grid))
    half = list(range(grid // 2))
    parts = []
    for yp in (0, 1):
        for zp in (0, 1):
            parts.append(np.kron(real_basis(grid, yp, freqs, points), real_basis(grid, zp, half, zline)).T)
    return np.concatenate(parts, axis=1)


def tables(grid):
    eighth = list(range(grid // 4))
    quarter = groups(grid)
    a = plane_table(grid, quarter[0], eighth)
    b = plane_table(grid, quarter[1], eighth)
    odd_points = list(range(grid // 2))
    c = np.concatenate([plane_table(grid, quarter[2], odd_points), plane_table(grid, quarter[3], odd_points)], axis=1)
    half = list(range(grid // 2))
    line = list(range(grid))
    x = np.concatenate([real_basis(grid, 0, half, line), real_basis(grid, 1, half, line)], axis=0)
    x_sides = np.zeros(a.shape, jnp.bfloat16)
    for at, side in enumerate((x, x.T)):
        high, low = split(np.kron(np.eye(2), side))
        x_sides[at * 2 * grid : (at + 1) * 2 * grid, : 6 * grid] = np.concatenate([high, low, high], axis=1)
    small = np.stack([t for m in (a, a.T, b, b.T) for t in split(m)] + [x_sides])
    large = np.stack([t for m in (c, c.T) for t in split(m)])
    return small, large


def lane_freqs(grid):
    half, count = grid // 2, grid // 8
    shape = (4, 1, 4 * count * half)
    quarter = lax.broadcasted_iota(jnp.int32, shape, 0)
    lane = lax.broadcasted_iota(jnp.int32, shape, 2)
    at = (lane // half) % count
    y = jnp.where(quarter < 2, 4 * at + 2 * quarter, 2 * at + 1 + 2 * count * (quarter - 2))
    z = lane % half
    found = []
    for size, second in ((y, lane // (2 * count * half) > 0), (z, (lane // (count * half)) % 2 > 0)):
        freq = jnp.where(second, jnp.where(size == 0, -half, -size), size)
        found.append((freq.astype(jnp.float32), jnp.where(size == 0, 0.0, 1.0).astype(jnp.float32)))
    return found


def halves(a):
    high = a.astype(jnp.bfloat16)
    low = (a - high.astype(jnp.float32)).astype(jnp.bfloat16)
    return high, low


def dot(a, b):
    return jnp.dot(a, b, preferred_element_type=jnp.float32)


def right(a, high_table, low_table):
    high, low = halves(a)
    rows = a.shape[0]
    both = dot(jnp.concatenate([high, low], axis=0), high_table)
    return both[:rows] + (both[rows:] + dot(high, low_table))


def left(side, a):
    high, low = halves(a)
    rows = side.shape[0]
    done = []
    for at in range(0, a.shape[0], rows):
        cut = slice(at, at + rows)
        done.append(dot(side, jnp.concatenate([high[cut], high[cut], low[cut]], axis=0)))
    return jnp.concatenate(done, axis=0)


def x_freq(grid, shape):
    half = grid // 2
    row = lax.broadcasted_iota(jnp.int32, shape, len(shape) - 2)
    freq = jnp.where(row < half, row, jnp.where(row == half, -half, half - row))
    return freq.astype(jnp.float32), jnp.where(row % half == 0, 0.0, 1.0).astype(jnp.float32)


def swap_x(a):
    half = a.shape[1] // 2
    return jnp.concatenate([a[:, half:], a[:, :half]], axis=1)


def swap_y(a):
    half = a.shape[2] // 2
    return jnp.concatenate([a[:, :, half:], a[:, :, :half]], axis=2)


def swap_z(a):
    half = a.shape[2] // 2
    parts = [pltpu.roll(a[:, :, at * half : (at + 1) * half], half // 2, 2) for at in (0, 1)]
    return jnp.concatenate(parts, axis=2)


def pairing_butterflies(field, paired, sign):
    re, im = field
    for swap, mask in zip((swap_x, swap_y, swap_z), paired):
        mask = sign * mask
        re, im = re + mask * swap(im), im - mask * swap(re)
    return re, im


def convolve(parts, kerns, small, large, paired):
    lanes = parts[0].shape[1]
    rows = parts[0].shape[0] // len(kerns)
    grid = rows // 2
    sum_02, sum_13 = parts[0] + parts[2], parts[1] + parts[3]
    odd = jnp.concatenate([parts[0] - parts[2], parts[1] - parts[3]], axis=1)
    freq_a = right(sum_02 + sum_13, small[0], small[1])
    freq_b = right(sum_02 - sum_13, small[4], small[5])
    freq_c = right(odd, large[0], large[1])
    fields = []
    for at, (kern, shifted) in enumerate(kerns):
        cut = slice(at * rows, (at + 1) * rows)
        field = jnp.concatenate([freq_a[cut], freq_b[cut], freq_c[cut, :lanes], freq_c[cut, lanes:]], axis=0)
        field = left(small[8, :rows, : 3 * rows], field).reshape(4, 2, grid, lanes)
        if shifted:
            re, im = pairing_butterflies((field[:, 0], field[:, 1]), paired, 1.0)
            re, im = pairing_butterflies((re * kern, im * kern), paired, -1.0)
            field = jnp.stack([re, im], axis=1)
        else:
            field = field * kern[:, None]
        fields.append(left(small[8, rows : 2 * rows, : 3 * rows], field.reshape(4 * rows, lanes)))
    quarters = [jnp.concatenate([f[q * rows : (q + 1) * rows] for f in fields], axis=0) for q in range(4)]
    back_a = right(quarters[0], small[2], small[3])
    back_b = right(quarters[1], small[6], small[7])
    back_c = right(jnp.concatenate(quarters[2:], axis=1), large[2], large[3])
    even, alternate = back_a + back_b, back_a - back_b
    return [even + back_c[:, :lanes], alternate + back_c[:, lanes:], even - back_c[:, :lanes], alternate - back_c[:, lanes:]]


def band_shifts(bands):
    counts = {}
    for shift in (1, -1, 2, -2):
        counts[shift % bands] = counts.get(shift % bands, 0) + 1
    return counts


def kernel(bands, kpts, times, kcoord_hbm, own_hbm, small_hbm, large_hbm, out_ref, kcoord_ref, own, got, small, large, local_sems, send_sems, recv_sems):
    band = lax.axis_index("band")
    kpt = lax.axis_index("kpt")
    later, earlier = (kpt + 1) % kpts, (kpt + kpts - 1) % kpts
    greeted = [(band, later)] + ([(band, earlier)] if kpts > 2 else [])
    if bands == 4:
        flip = (band + 1 - 2 * (band % 2), kpt)
        across = ((band + 2) % 4, kpt)
        greeted += [flip, across, (3 - band, kpt)]
    else:
        greeted += [((band + shift) % bands, kpt) for shift in band_shifts(bands)]

    barrier = pltpu.get_barrier_semaphore()
    for device in greeted:
        pl.semaphore_signal(barrier, inc=1, device_id=device, device_id_type=MESH)
    fetches = [
        pltpu.make_async_copy(own_hbm, own, local_sems.at[0]),
        pltpu.make_async_copy(small_hbm, small, local_sems.at[1]),
        pltpu.make_async_copy(large_hbm, large, local_sems.at[2]),
        pltpu.make_async_copy(kcoord_hbm, kcoord_ref, local_sems.at[3]),
    ]
    for fetch in fetches:
        fetch.start()
    pl.semaphore_wait(barrier, len(greeted))
    sent = []

    def send(src, dst, device):
        at = len(sent)
        copy = pltpu.make_async_remote_copy(
            src_ref=src,
            dst_ref=dst,
            send_sem=send_sems.at[at],
            recv_sem=recv_sems.at[at],
            device_id=device,
            device_id_type=MESH,
        )
        copy.start()
        sent.append(copy)
        return copy

    if bands == 4:
        corner = (3 - band, kpt)
        awaited = {at: [send(own_hbm, got.at[at], device)] for at, device in ((1, flip), (2, across), (0, (band, earlier)), (3, corner))}
        groups_of = [[0], [1, 2], [3]]
    else:
        awaited = {0: [send(own_hbm, got.at[0], (band, earlier))]}
        for at, shift in enumerate(band_shifts(bands)):
            awaited[at + 1] = [send(own_hbm, got.at[at + 1], ((band + bands - shift) % bands, kpt))]
        groups_of = [[0], list(range(1, len(times)))]

    grid = own_hbm.shape[1]
    lanes = own_hbm.shape[2] // 4
    scale = -1.0 / float(grid**3)
    fx, x_paired = x_freq(grid, (1, grid, lanes))
    (fy, y_paired), (fz, z_paired) = lane_freqs(grid)
    for fetch in fetches:
        fetch.wait()
    qx, qy, qz = [(kcoord_ref[i, later] - kcoord_ref[i, kpt]).astype(jnp.float32) for i in range(3)]
    weight = (1.0 + x_paired) * ((1.0 + y_paired) * (1.0 + z_paired)) * scale
    kern_zero = weight / (1.0 + (fx * fx + fy * fy + fz * fz) / 256.0)
    gx, gy, gz = fx + qx, fy + qy, fz + qz
    kern_next = scale / (1.0 + (gx * gx + gy * gy + gz * gz) / 256.0)

    rows = 2 * grid
    for group in groups_of:
        for at in group:
            for copy in awaited[at]:
                copy.wait_recv()
        parts = []
        for part in range(4):
            cut = slice(part * lanes, (part + 1) * lanes)
            own_re, own_im = own[0, :, cut].astype(jnp.float32), own[1, :, cut].astype(jnp.float32)
            rho = []
            for at in group:
                re, im = got[at, 0, :, cut].astype(jnp.float32), got[at, 1, :, cut].astype(jnp.float32)
                rho += [re * own_re + im * own_im, re * own_im - im * own_re]
            parts.append(jnp.concatenate(rho, axis=0))
        kerns = [(kern_zero * times[at], False) if at > 0 else (kern_next, True) for at in group]
        phi = convolve(parts, kerns, small, large, (x_paired, y_paired, z_paired))
        for part in range(4):
            cut = slice(part * lanes, (part + 1) * lanes)
            total_re, total_im = [], []
            if group != groups_of[0]:
                total_re, total_im = [out_ref[0, :, cut]], [out_ref[1, :, cut]]
            for place, at in enumerate(group):
                re, im = got[at, 0, :, cut].astype(jnp.float32), got[at, 1, :, cut].astype(jnp.float32)
                phi_re = phi[part][place * rows : place * rows + grid]
                phi_im = phi[part][place * rows + grid : (place + 1) * rows]
                total_re.append(re * phi_re - im * phi_im)
                total_im.append(re * phi_im + im * phi_re)
            out_ref[0, :, cut] = sum(total_re[1:], total_re[0])
            out_ref[1, :, cut] = sum(total_im[1:], total_im[0])
    for copy in sent:
        copy.wait_send()


def local(bands, kpts, orbitals, kcoord):
    own = orbitals[0, 0]
    grid, merged = own.shape[1:]
    small, large = tables(grid)
    counts = band_shifts(bands)
    times = [1.0, 1.0, 2.0, 1.0] if bands == 4 else [1.0] + [float(c) for c in counts.values()]
    sends = len(times)
    hbm = pl.BlockSpec(memory_space=pltpu.HBM)
    vmem = pl.BlockSpec(memory_space=pltpu.VMEM)
    out = pl.pallas_call(
        functools.partial(kernel, bands, kpts, times),
        out_shape=pltpu.VMEM((2, grid, merged), jnp.float32),
        in_specs=[hbm, hbm, hbm, hbm],
        out_specs=vmem,
        scratch_shapes=[
            pltpu.SMEM(kcoord.T.shape, jnp.int32),
            pltpu.VMEM(own.shape, jnp.bfloat16),
            pltpu.VMEM((len(times), *own.shape), jnp.bfloat16),
            pltpu.VMEM(small.shape, jnp.bfloat16),
            pltpu.VMEM(large.shape, jnp.bfloat16),
            pltpu.SemaphoreType.DMA((4,)),
            pltpu.SemaphoreType.DMA((sends,)),
            pltpu.SemaphoreType.DMA((sends,)),
        ],
        compiler_params=pltpu.CompilerParams(collective_id=0, has_side_effects=True, vmem_limit_bytes=VMEM_BYTES),
    )(kcoord.T, own, jnp.asarray(small), jnp.asarray(large))
    return out.reshape(1, 1, 2, grid, merged)


def solution(mesh):
    in_specs = (P("band", "kpt", None, None, None), P())
    out_specs = P("band", "kpt", None, None, None)
    body = functools.partial(local, mesh.shape["band"], mesh.shape["kpt"])
    return jax.shard_map(body, mesh=mesh, in_specs=in_specs, out_specs=out_specs, check_vma=False)
```

```python
import functools
import math

import jax
import jax.numpy as jnp
import numpy as np
from jax import lax
from jax.experimental import pallas as pl
from jax.experimental.pallas import tpu as pltpu
from jax.sharding import PartitionSpec as P

MESH = pl.DeviceIdType.MESH
VMEM_BYTES = 56 * 1024 * 1024


def real_basis(grid, parity, freqs, points):
    angle = 2.0 * math.pi / grid * (np.outer(freqs, points) % grid)
    if parity == 0:
        return np.cos(angle)
    rows = np.sin(angle)
    for at, freq in enumerate(freqs):
        if freq == 0:
            rows[at] = np.cos(math.pi * np.asarray(points))
    return rows


def split(table):
    table = np.asarray(table, np.float32)
    high = table.astype(jnp.bfloat16)
    low = (table - high.astype(np.float32)).astype(jnp.bfloat16)
    return [high, low]


def groups(grid):
    half = grid // 2
    odd = list(range(1, half, 2))
    return [list(range(0, half, 4)), list(range(2, half, 4)), odd[: len(odd) // 2], odd[len(odd) // 2 :]]


def plane_table(grid, freqs, points):
    zline = list(range(grid))
    half = list(range(grid // 2))
    parts = []
    for yp in (0, 1):
        for zp in (0, 1):
            parts.append(np.kron(real_basis(grid, yp, freqs, points), real_basis(grid, zp, half, zline)).T)
    return np.concatenate(parts, axis=1)


def tables(grid):
    eighth = list(range(grid // 4))
    quarter = groups(grid)
    a = plane_table(grid, quarter[0], eighth)
    b = plane_table(grid, quarter[1], eighth)
    odd_points = list(range(grid // 2))
    c = np.concatenate([plane_table(grid, quarter[2], odd_points), plane_table(grid, quarter[3], odd_points)], axis=1)
    half = list(range(grid // 2))
    line = list(range(grid))
    x = np.concatenate([real_basis(grid, 0, half, line), real_basis(grid, 1, half, line)], axis=0)
    x_sides = np.zeros(a.shape, jnp.bfloat16)
    for at, side in enumerate((x, x.T)):
        high, low = split(np.kron(np.eye(2), side))
        x_sides[at * 2 * grid : (at + 1) * 2 * grid, : 6 * grid] = np.concatenate([high, low, high], axis=1)
    small = np.stack([t for m in (a, a.T, b, b.T) for t in split(m)] + [x_sides])
    large = np.stack([t for m in (c, c.T) for t in split(m)])
    return small, large


def lane_freqs(grid):
    half, count = grid // 2, grid // 8
    shape = (4, 1, 4 * count * half)
    quarter = lax.broadcasted_iota(jnp.int32, shape, 0)
    lane = lax.broadcasted_iota(jnp.int32, shape, 2)
    at = (lane // half) % count
    y = jnp.where(quarter < 2, 4 * at + 2 * quarter, 2 * at + 1 + 2 * count * (quarter - 2))
    z = lane % half
    found = []
    for size, second in ((y, lane // (2 * count * half) > 0), (z, (lane // (count * half)) % 2 > 0)):
        freq = jnp.where(second, jnp.where(size == 0, -half, -size), size)
        found.append((freq.astype(jnp.float32), jnp.where(size == 0, 0.0, 1.0).astype(jnp.float32)))
    return found


def halves(a):
    high = a.astype(jnp.bfloat16)
    low = (a - high.astype(jnp.float32)).astype(jnp.bfloat16)
    return high, low


def dot(a, b):
    return jnp.dot(a, b, preferred_element_type=jnp.float32)


def right(a, high_table, low_table):
    high, low = halves(a)
    rows = a.shape[0]
    both = dot(jnp.concatenate([high, low], axis=0), high_table)
    return both[:rows] + (both[rows:] + dot(high, low_table))


def left(side, a):
    high, low = halves(a)
    rows = side.shape[0]
    done = []
    for at in range(0, a.shape[0], rows):
        cut = slice(at, at + rows)
        done.append(dot(side, jnp.concatenate([high[cut], high[cut], low[cut]], axis=0)))
    return jnp.concatenate(done, axis=0)


def x_freq(grid, shape):
    half = grid // 2
    row = lax.broadcasted_iota(jnp.int32, shape, len(shape) - 2)
    freq = jnp.where(row < half, row, jnp.where(row == half, -half, half - row))
    return freq.astype(jnp.float32), jnp.where(row % half == 0, 0.0, 1.0).astype(jnp.float32)


def swap_x(a):
    half = a.shape[1] // 2
    return jnp.concatenate([a[:, half:], a[:, :half]], axis=1)


def swap_y(a):
    half = a.shape[2] // 2
    return jnp.concatenate([a[:, :, half:], a[:, :, :half]], axis=2)


def swap_z(a):
    half = a.shape[2] // 2
    parts = [pltpu.roll(a[:, :, at * half : (at + 1) * half], half // 2, 2) for at in (0, 1)]
    return jnp.concatenate(parts, axis=2)


def pairing_butterflies(field, paired, sign):
    re, im = field
    for swap, mask in zip((swap_x, swap_y, swap_z), paired):
        mask = sign * mask
        re, im = re + mask * swap(im), im - mask * swap(re)
    return re, im


def convolve(parts, kerns, small, large, paired):
    lanes = parts[0].shape[1]
    rows = parts[0].shape[0] // len(kerns)
    grid = rows // 2
    sum_02, sum_13 = parts[0] + parts[2], parts[1] + parts[3]
    odd = jnp.concatenate([parts[0] - parts[2], parts[1] - parts[3]], axis=1)
    freq_a = right(sum_02 + sum_13, small[0], small[1])
    freq_b = right(sum_02 - sum_13, small[4], small[5])
    freq_c = right(odd, large[0], large[1])
    fields = []
    for at, (kern, shifted) in enumerate(kerns):
        cut = slice(at * rows, (at + 1) * rows)
        field = jnp.concatenate([freq_a[cut], freq_b[cut], freq_c[cut, :lanes], freq_c[cut, lanes:]], axis=0)
        field = left(small[8, :rows, : 3 * rows], field).reshape(4, 2, grid, lanes)
        if shifted:
            re, im = pairing_butterflies((field[:, 0], field[:, 1]), paired, 1.0)
            re, im = pairing_butterflies((re * kern, im * kern), paired, -1.0)
            field = jnp.stack([re, im], axis=1)
        else:
            field = field * kern[:, None]
        fields.append(left(small[8, rows : 2 * rows, : 3 * rows], field.reshape(4 * rows, lanes)))
    quarters = [jnp.concatenate([f[q * rows : (q + 1) * rows] for f in fields], axis=0) for q in range(4)]
    back_a = right(quarters[0], small[2], small[3])
    back_b = right(quarters[1], small[6], small[7])
    back_c = right(jnp.concatenate(quarters[2:], axis=1), large[2], large[3])
    even, alternate = back_a + back_b, back_a - back_b
    return [even + back_c[:, :lanes], alternate + back_c[:, lanes:], even - back_c[:, :lanes], alternate - back_c[:, lanes:]]


def band_shifts(bands):
    counts = {}
    for shift in (1, -1, 2, -2):
        counts[shift % bands] = counts.get(shift % bands, 0) + 1
    return counts


def kernel(bands, kpts, times, kcoord_hbm, own_hbm, small_hbm, large_hbm, out_ref, kcoord_ref, own, got, small, large, local_sems, send_sems, recv_sems):
    band = lax.axis_index("band")
    kpt = lax.axis_index("kpt")
    later, earlier = (kpt + 1) % kpts, (kpt + kpts - 1) % kpts
    greeted = [(band, later)] + ([(band, earlier)] if kpts > 2 else [])
    if bands == 4:
        flip = (band + 1 - 2 * (band % 2), kpt)
        across = ((band + 2) % 4, kpt)
        greeted += [flip, across, (3 - band, kpt)]
    else:
        greeted += [((band + shift) % bands, kpt) for shift in band_shifts(bands)]

    barrier = pltpu.get_barrier_semaphore()
    for device in greeted:
        pl.semaphore_signal(barrier, inc=1, device_id=device, device_id_type=MESH)
    fetches = [
        pltpu.make_async_copy(own_hbm, own, local_sems.at[0]),
        pltpu.make_async_copy(small_hbm, small, local_sems.at[1]),
        pltpu.make_async_copy(large_hbm, large, local_sems.at[2]),
        pltpu.make_async_copy(kcoord_hbm, kcoord_ref, local_sems.at[3]),
    ]
    for fetch in fetches:
        fetch.start()
    pl.semaphore_wait(barrier, len(greeted))
    sent = []
    fetches[0].wait()

    def send(src, dst, device):
        at = len(sent)
        copy = pltpu.make_async_remote_copy(
            src_ref=src,
            dst_ref=dst,
            send_sem=send_sems.at[at],
            recv_sem=recv_sems.at[at],
            device_id=device,
            device_id_type=MESH,
        )
        copy.start()
        sent.append(copy)
        return copy

    if bands == 4:
        corner = (3 - band, kpt)
        half = own_hbm.shape[1] // 2
        first, second = slice(0, half), slice(half, 2 * half)
        by_flip = send(own.at[1, first], got.at[1, 1, first], flip)
        by_across = send(own.at[1, second], got.at[2, 1, second], across)
        awaited = {
            1: [send(own.at[0], got.at[1, 0], flip), send(own.at[1, second], got.at[1, 1, second], flip)],
            2: [send(own.at[0], got.at[2, 0], across), send(own.at[1, first], got.at[2, 1, first], across)],
            0: [send(own, got.at[0], (band, earlier))],
            3: [send(own.at[0], got.at[3, 0], corner)],
        }
        groups_of = [[0], [1, 2], [3]]
    else:
        awaited = {0: [send(own, got.at[0], (band, earlier))]}
        for at, shift in enumerate(band_shifts(bands)):
            awaited[at + 1] = [send(own, got.at[at + 1], ((band + bands - shift) % bands, kpt))]
        groups_of = [[0], list(range(1, len(times)))]

    grid = own_hbm.shape[1]
    lanes = own_hbm.shape[2] // 4
    scale = -1.0 / float(grid**3)
    fx, x_paired = x_freq(grid, (1, grid, lanes))
    (fy, y_paired), (fz, z_paired) = lane_freqs(grid)
    for fetch in fetches[1:]:
        fetch.wait()
    qx, qy, qz = [(kcoord_ref[i, later] - kcoord_ref[i, kpt]).astype(jnp.float32) for i in range(3)]
    weight = (1.0 + x_paired) * ((1.0 + y_paired) * (1.0 + z_paired)) * scale
    kern_zero = weight / (1.0 + (fx * fx + fy * fy + fz * fz) / 256.0)
    gx, gy, gz = fx + qx, fy + qy, fz + qz
    kern_next = scale / (1.0 + (gx * gx + gy * gy + gz * gz) / 256.0)

    if bands == 4:
        by_flip.wait_recv()
        awaited[3].append(send(got.at[1, 1, first], got.at[3, 1, first], across))
        by_across.wait_recv()
        awaited[3].append(send(got.at[2, 1, second], got.at[3, 1, second], flip))
    rows = 2 * grid
    for group in groups_of:
        for at in group:
            for copy in awaited[at]:
                copy.wait_recv()
        parts = []
        for part in range(4):
            cut = slice(part * lanes, (part + 1) * lanes)
            own_re, own_im = own[0, :, cut].astype(jnp.float32), own[1, :, cut].astype(jnp.float32)
            rho = []
            for at in group:
                re, im = got[at, 0, :, cut].astype(jnp.float32), got[at, 1, :, cut].astype(jnp.float32)
                rho += [re * own_re + im * own_im, re * own_im - im * own_re]
            parts.append(jnp.concatenate(rho, axis=0))
        kerns = [(kern_zero * times[at], False) if at > 0 else (kern_next, True) for at in group]
        phi = convolve(parts, kerns, small, large, (x_paired, y_paired, z_paired))
        for part in range(4):
            cut = slice(part * lanes, (part + 1) * lanes)
            total_re, total_im = [], []
            if group != groups_of[0]:
                total_re, total_im = [out_ref[0, :, cut]], [out_ref[1, :, cut]]
            for place, at in enumerate(group):
                re, im = got[at, 0, :, cut].astype(jnp.float32), got[at, 1, :, cut].astype(jnp.float32)
                phi_re = phi[part][place * rows : place * rows + grid]
                phi_im = phi[part][place * rows + grid : (place + 1) * rows]
                total_re.append(re * phi_re - im * phi_im)
                total_im.append(re * phi_im + im * phi_re)
            out_ref[0, :, cut] = sum(total_re[1:], total_re[0])
            out_ref[1, :, cut] = sum(total_im[1:], total_im[0])
    for copy in sent:
        copy.wait_send()


def local(bands, kpts, orbitals, kcoord):
    own = orbitals[0, 0]
    grid, merged = own.shape[1:]
    small, large = tables(grid)
    counts = band_shifts(bands)
    times = [1.0, 1.0, 2.0, 1.0] if bands == 4 else [1.0] + [float(c) for c in counts.values()]
    sends = 10 if bands == 4 else len(times)
    hbm = pl.BlockSpec(memory_space=pltpu.HBM)
    vmem = pl.BlockSpec(memory_space=pltpu.VMEM)
    out = pl.pallas_call(
        functools.partial(kernel, bands, kpts, times),
        out_shape=pltpu.VMEM((2, grid, merged), jnp.float32),
        in_specs=[hbm, hbm, hbm, hbm],
        out_specs=vmem,
        scratch_shapes=[
            pltpu.SMEM(kcoord.T.shape, jnp.int32),
            pltpu.VMEM(own.shape, jnp.bfloat16),
            pltpu.VMEM((len(times), *own.shape), jnp.bfloat16),
            pltpu.VMEM(small.shape, jnp.bfloat16),
            pltpu.VMEM(large.shape, jnp.bfloat16),
            pltpu.SemaphoreType.DMA((4,)),
            pltpu.SemaphoreType.DMA((sends,)),
            pltpu.SemaphoreType.DMA((sends,)),
        ],
        compiler_params=pltpu.CompilerParams(collective_id=0, has_side_effects=True, vmem_limit_bytes=VMEM_BYTES),
    )(kcoord.T, own, jnp.asarray(small), jnp.asarray(large))
    return out.reshape(1, 1, 2, grid, merged)


def solution(mesh):
    in_specs = (P("band", "kpt", None, None, None), P())
    out_specs = P("band", "kpt", None, None, None)
    body = functools.partial(local, mesh.shape["band"], mesh.shape["kpt"])
    return jax.shard_map(body, mesh=mesh, in_specs=in_specs, out_specs=out_specs, check_vma=False)
```
